32 devices in a mesh: row: 4 (over z), col: 8 (over y, x, core).
Axes of the slice: x: 2, y: 2, z: 4, core: 2. Of those that a mesh axis runs over, the one named last changes fastest.
Arguments:
- v_coef: float32 [2, 512, 768, 256], P(None, 'col', 'row'), may hold values from -0.75 to 0.75
- vort_coef: float32 [2, 512, 768, 256], P(None, 'col', 'row'), may hold values from -6 to 6
- plane_ops: float32 [3, 12, 256], replicated, may hold values from -0.375 to 0.375
- inverse_ops: float32 [2, 256, 12], replicated, may hold values from -1.75 to 1.75
Outputs:
- vort_rhs: float32 [2, 512, 768, 256], P(None, 'col', 'row')
- lapv_rhs: float32 [2, 512, 768, 256], P(None, 'col', 'row')
The draws below stay inside these ranges and needn't reach their ends.
All inputs are finite; a program needn't handle non-finite values.
Results may differ from the reference program's by a relative error of at most 0.00012.
Values sent between devices are 32-bit elements; how exact they have to be, the bound alone decides.
A program may use at most 192 MiB of HBM per device.

```python
import jax
import jax.numpy as jnp
from jax import lax

KX = 512
KZ = 768
NY = 256
PLANES = 12


def spectrum(key, amplitude):
    stream_modes = jnp.arange(KX, dtype=jnp.int32).astype(jnp.float32) * 0.25
    span_index = jnp.arange(KZ, dtype=jnp.int32)
    signed = jnp.where(span_index < KZ // 2, span_index, span_index - KZ).astype(jnp.float32) * (2.0 / 3.0)
    square = stream_modes[:, None] * stream_modes[:, None] + signed[None, :] * signed[None, :]
    shaping = amplitude / (1.0 + square / 256.0)
    gaussian = jax.random.truncated_normal(key, -6.0, 6.0, (2, KX, KZ, NY), jnp.float32)
    return gaussian * shaping[None, :, :, None]


def draw_v_coef(key, part):
    return spectrum(jax.random.fold_in(key, 3), 0.125)


def draw_vort_coef(key, part):
    return spectrum(jax.random.fold_in(key, 7), 1.0)


def bell_draw(rng, extent, spread, reach, kind=jnp.bfloat16):
    return jnp.clip(spread * jax.random.normal(rng, extent, jnp.float32), -reach, reach).astype(kind)


def setup_inputs(seed: int = 0) -> dict:
    arg_keys = jax.random.split(jax.random.key(seed), 5)
    return {
        "v_coef": draw_v_coef(jax.random.fold_in(arg_keys[4], 71), 0),
        "vort_coef": draw_vort_coef(jax.random.fold_in(arg_keys[4], 71), 0),
        "plane_ops": bell_draw(arg_keys[2], (3, PLANES, NY), NY ** -0.5, 0.375, jnp.float32),
        "inverse_ops": bell_draw(arg_keys[3], (2, NY, PLANES), PLANES ** -0.5, 1.75, jnp.float32),
    }


PRECISE = lax.Precision.HIGHEST
STREAM_STEP = 0.25
SPAN_STEP = 2.0 / 3.0
INVERSE_SCALE = 1.0 / 32.0
FORWARD_SCALE = 32.0

def reference(v_coef, vort_coef, plane_ops, inverse_ops):
    points_x = 3 * KX
    points_z = 3 * KZ // 2
    half = KZ // 2
    stream = (STREAM_STEP * jnp.arange(KX, dtype=jnp.int32).astype(jnp.float32))[:, None]
    span_index = jnp.arange(KZ, dtype=jnp.int32)
    signed = jnp.where(span_index < half, span_index, span_index - KZ)
    span = (SPAN_STEP * signed.astype(jnp.float32))[None, :]
    square = stream * stream + span * span
    recip = 1.0 / jnp.where(square > 0, square, 1.0)
    v_values = jnp.einsum('rpj,cxkj->rpcxk', plane_ops, v_coef, precision=PRECISE)
    g_values = jnp.einsum('rpj,cxkj->rpcxk', plane_ops[:2], vort_coef, precision=PRECISE)
    v_cplx = v_values[:, :, 0] + 1j * v_values[:, :, 1]
    g_cplx = g_values[:, :, 0] + 1j * g_values[:, :, 1]
    v_base, v_slope, v_curve = (v_cplx[0], v_cplx[1], v_cplx[2])
    g_base, g_slope = (g_cplx[0], g_cplx[1])
    along = (1j * stream * v_slope - 1j * span * g_base) * recip
    across = (1j * span * v_slope + 1j * stream * g_base) * recip
    omega_x = (1j * span * v_curve + 1j * stream * g_slope) * recip - 1j * span * v_base
    omega_z = 1j * stream * v_base - (1j * stream * v_curve - 1j * span * g_slope) * recip
    fields = jnp.stack([along, v_base, across, omega_x, g_base, omega_z], axis=1)

    def one_plane(slab):
        padded = jnp.zeros((6, KX, points_z), slab.dtype)
        padded = padded.at[:, :, :half].set(slab[:, :, :half])
        padded = padded.at[:, :, points_z - half:].set(slab[:, :, half:])
        span_phys = jnp.fft.ifft(padded, axis=-1) * points_z
        wide = jnp.zeros((6, points_x // 2 + 1, points_z), slab.dtype)
        wide = wide.at[:, :KX].set(span_phys)
        physical_space = jnp.fft.irfft(wide, n=points_x, axis=1) * (points_x * INVERSE_SCALE)
        velocity_field = physical_space[0:3]
        vorticity_field = physical_space[3:6]
        product_streamwise = velocity_field[1] * vorticity_field[2] - velocity_field[2] * vorticity_field[1]
        product_normal = velocity_field[2] * vorticity_field[0] - velocity_field[0] * vorticity_field[2]
        product_spanwise = velocity_field[0] * vorticity_field[1] - velocity_field[1] * vorticity_field[0]
        products = jnp.stack([product_streamwise, product_normal, product_spanwise], axis=0)
        stream_spec = jnp.fft.rfft(products, axis=1)[:, :KX] / points_x
        full_spec = jnp.fft.fft(stream_spec, axis=-1) * (FORWARD_SCALE / points_z)
        return jnp.concatenate([full_spec[:, :, :half], full_spec[:, :, points_z - half:]], axis=-1)
    spectral = lax.map(one_plane, fields)
    h_x, h_y, h_z = (spectral[:, 0], spectral[:, 1], spectral[:, 2])
    g_term = 1j * span * h_x - 1j * stream * h_z
    s_term = -(1j * stream * h_x + 1j * span * h_z)
    y_term = -square * h_y
    damp_g = 1.0 / jnp.sqrt(1.0 + square)
    damp_v = 1.0 / (1.0 + square)

    def contract(matrix, term):
        real_part = jnp.einsum('jp,pxk->xkj', matrix, jnp.real(term), precision=PRECISE)
        imag_part = jnp.einsum('jp,pxk->xkj', matrix, jnp.imag(term), precision=PRECISE)
        return jnp.stack([real_part, imag_part], axis=0)
    vort_rhs = contract(inverse_ops[0], g_term) * damp_g[None, :, :, None]
    lapv_sum = contract(inverse_ops[1], s_term) + contract(inverse_ops[0], y_term)
    lapv_rhs = lapv_sum * damp_v[None, :, :, None]
    return (vort_rhs, lapv_rhs)
```

```python
import functools
import math

import jax
import jax.numpy as jnp
import ml_dtypes
import numpy as np
from jax import lax
from jax.experimental import pallas as pl
from jax.experimental.pallas import tpu as pltpu
from jax.sharding import PartitionSpec as P

PRECISE = lax.Precision.HIGHEST
STREAM_STEP = 0.25
SPAN_STEP = 2.0 / 3.0
INVERSE_SCALE = 1.0 / 32.0
FORWARD_SCALE = 32.0
LANES = 128
VMEM_LIMIT = 44 * 1024 * 1024
MESH = pl.DeviceIdType.MESH
F32 = jnp.float32
BF16 = jnp.bfloat16


def halves(table):
    table = np.asarray(table, np.float32)
    high = table.astype(ml_dtypes.bfloat16)
    low = (table - high.astype(np.float32)).astype(ml_dtypes.bfloat16)
    return np.stack([high, low], axis=0)


def signed_order(rows, span_local, span_total):
    n = (
        span_local * np.arange(rows)[:, None, None]
        + np.arange(2)[None, :, None]
        + 2 * np.arange(span_local // 2)[None, None, :]
    )
    return np.where(n < span_total // 2, n, n - span_total)


def span_fast_tables(rows, span_local, span_total):
    points = 3 * span_total // 2
    signed = signed_order(rows, span_local, span_total)
    grid = np.arange(points // 2)
    inverse, forward = [], []
    for parity in range(2):
        s = signed[:, parity, :].reshape(-1)
        angle = np.mod(s[None, :] * grid[:, None], points) * (2.0 * math.pi / points)
        inverse.append(np.concatenate([np.cos(angle), np.sin(angle)], axis=1))
        factor = FORWARD_SCALE / points
        forward.append(np.concatenate([np.cos(angle).T, np.sin(angle).T], axis=1) * factor)
    return halves(np.stack(inverse)), halves(np.stack(forward))


def stream_fast_tables(total):
    points = 3 * total
    grid = np.arange(points // 4) + 0.5
    inverse, forward = [], []
    for part in range(2):
        for parity in range(2):
            m = 2 * np.arange(total // 2) + parity
            angle = np.mod(m[:, None] * grid[None, :], points) * (2.0 * math.pi / points)
            wave = np.cos(angle) if part == 0 else -np.sin(angle)
            weight = np.where(m == 0, 1.0, 2.0)[:, None]
            inverse.append(weight * wave * INVERSE_SCALE)
            forward.append(wave.T / points)
    return halves(np.stack(inverse)), halves(np.stack(forward))


def split(values):
    high = values.astype(BF16)
    return high, (values - high.astype(F32)).astype(BF16)


def dot(a, b):
    return jnp.dot(a, b, preferred_element_type=F32)


def dot3(a_high, a_low, b_high, b_low):
    return dot(a_high, b_high) + (dot(a_high, b_low) + dot(a_low, b_high))


def times_i(values):
    axis = values.ndim - 1
    lane = lax.broadcasted_iota(jnp.int32, values.shape, axis)
    turned = pltpu.roll(values, LANES // 2, axis)
    return jnp.where(lane < LANES // 2, -turned, turned)


def block_transpose(a):
    lane = lax.broadcasted_iota(jnp.int32, a[0].shape, 1)
    left = lane < 64
    odd = (lane // 32) % 2 == 1
    t = [None] * 4
    for s in range(2):
        t[s] = jnp.where(left, a[s], pltpu.roll(a[s + 2], 64, 1))
        t[s + 2] = jnp.where(left, pltpu.roll(a[s], 64, 1), a[s + 2])
    out = [None] * 4
    for s in (0, 2):
        out[s] = jnp.where(odd, pltpu.roll(t[s + 1], 32, 1), t[s])
        out[s + 1] = jnp.where(odd, t[s + 1], pltpu.roll(t[s], 96, 1))
    return out


def contract_last(a, b):
    return lax.dot_general(a, b, (((1,), (1,)), ((), ())), preferred_element_type=F32)


def plane_kernel(v0, v1, g0, g1, wv_ref, wg_ref, out_ref, *, count):
    flat = out_ref.reshape(out_ref.shape[0] * 16, LANES)
    base = 0
    for low_ref, high_ref, w_ref, ops in ((v0, v1, wv_ref, 3), (g0, g1, wg_ref, 2)):
        refs = [ref.reshape(2 * 64 * 16, LANES) for ref in (low_ref, high_ref)]
        pad = w_ref.shape[0] // 2
        for parity in range(2):
            for pair in range(4):
                rows = []
                for half in (2 * pair, 2 * pair + 1):
                    for part in range(2):
                        for odd in range(2):
                            start = part * 1024 + odd * 16 + 2 * half + parity
                            rows.append(
                                jnp.concatenate(
                                    [ref[pl.ds(start, 32, stride=32), :] for ref in refs], axis=1
                                )
                            )
                high, low = split(jnp.concatenate(rows, axis=0))
                first = contract_last(w_ref[...], high)
                second = contract_last(w_ref[:pad], low)
                sums = first[:pad] + (first[pad:] + second)
                used = ops * count
                for side in range(2):
                    at = base * 16 + parity * 8 + 2 * pair + side
                    flat[pl.ds(at, used, stride=16), :] = sums[
                        :used, side * LANES : (side + 1) * LANES
                    ]
        base += ops * count


def span_inverse_kernel(r_ref, kx_ref, kz_ref, t_ref, out_ref, high_ref, low_ref, *, rows, half):
    modes = rows * half

    @pl.when(pl.program_id(0) == 0)
    def _():
        kx = kx_ref[...]
        for row in range(rows):
            for parity in range(2):
                kz = kz_ref[row, parity]
                square = kx * kx + kz * kz
                recip = 1.0 / jnp.where(square > 0, square, 1.0)
                vb, vd, vdd, gb, gd = [r_ref[row, f, parity] for f in range(5)]
                members = [
                    times_i((kx * vd - kz * gb) * recip),
                    vb,
                    times_i((kz * vd + kx * gb) * recip),
                    times_i((kz * vdd + kx * gd) * recip - kz * vb),
                    gb,
                    times_i(kx * vb - (kx * vdd - kz * gd) * recip),
                ]
                for f, member in enumerate(members):
                    for place, values in ((0, member), (modes, times_i(member))):
                        high, low = split(values)
                        at = pl.ds(place + row * half, half)
                        high_ref[f // 2, parity, at, pl.ds((f % 2) * LANES, LANES)] = high
                        low_ref[f // 2, parity, at, pl.ds((f % 2) * LANES, LANES)] = low

    pair = pl.program_id(0)
    even, odd = [
        dot3(t_ref[0, q], t_ref[1, q], high_ref[pair, q], low_ref[pair, q]) for q in range(2)
    ]
    plus, minus = even + odd, even - odd
    dests = out_ref.shape[0]
    step = out_ref.shape[2] // 2
    for d in range(dests):
        for f in range(2):
            lanes = slice(f * LANES, (f + 1) * LANES)
            out_ref[d, f, :step] = plus[d * step : (d + 1) * step, lanes]
            out_ref[d, f, step:] = minus[d * step : (d + 1) * step, lanes]


def stream_kernel(x_ref, ti_ref, tf_ref, out_ref):
    sources, fields, block, _ = x_ref.shape
    width = ti_ref.shape[3]
    parts = [x_ref[s].reshape(fields * block, LANES) for s in range(sources)]
    groups = [[] for _ in range(4)]
    for s in range(0, sources, 4):
        for g, piece in enumerate(block_transpose(parts[s : s + 4])):
            groups[g].append(piece)
    spectral = []
    for g in range(4):
        high, low = split(jnp.concatenate(groups[g], axis=1))
        spectral.append(dot3(high, low, ti_ref[0, g], ti_ref[1, g]))
    ce, co, se, so = [s.reshape(fields, block, width) for s in spectral]
    a, b, c, d = ce + co, se + so, ce - co, se - so
    products = []
    for image in (a + b, a - b, c + d, c - d):
        u, v, w, ox, oy, oz = [image[f] for f in range(6)]
        products.append(jnp.stack([v * oz - w * oy, w * ox - u * oz, u * oy - v * ox], axis=0))
    h1, h2, h3, h4 = [h.reshape(3 * block, width) for h in products]
    sum1, sum2, dif1, dif2 = h1 + h2, h3 + h4, h1 - h2, h3 - h4
    results = []
    for g, h in enumerate((sum1 + sum2, sum1 - sum2, dif1 + dif2, dif1 - dif2)):
        high, low = split(h)
        results.append(dot3(high, low, tf_ref[0, g], tf_ref[1, g]))
    for s in range(0, sources, 4):
        at = (s // 4) * LANES
        pieces = block_transpose([r[:, at : at + LANES] for r in results])
        for k in range(4):
            out_ref[s + k] = pieces[k].reshape(3, block, LANES)


def span_forward_kernel(x_ref, t_ref, out_ref):
    sources, fields, both, _ = x_ref.shape
    step = both // 2
    rows, half = out_ref.shape[0], out_ref.shape[3]
    for parity in range(2):
        columns = []
        for f in range(fields):
            first, second = x_ref[:, f, :step], x_ref[:, f, step:]
            h = first + second if parity == 0 else first - second
            h = h.reshape(sources * step, LANES)
            columns.append(jnp.concatenate([h, -times_i(h)], axis=0))
        high, low = split(jnp.concatenate(columns, axis=1))
        result = dot3(t_ref[0, parity], t_ref[1, parity], high, low)
        for row in range(rows):
            for f in range(fields):
                out_ref[row, f, parity] = result[
                    row * half : (row + 1) * half, f * LANES : (f + 1) * LANES
                ]


def combine_kernel(*refs, chunks, rows, count):
    h_refs = refs[:chunks]
    kx_ref, kz_ref, w_ref, vort_ref, lapv_ref, terms, *sums = refs[chunks:]
    kx = kx_ref[...]
    padded = terms.shape[0] // 16
    if padded > 3 * count:
        terms[3 * count * 16 :, :] = jnp.zeros(((padded - 3 * count) * 16, LANES), F32)
    for parity in range(2):
        kz = kz_ref[parity]
        square = kx * kx + kz * kz
        damp_g = 1.0 / jnp.sqrt(1.0 + square)
        damp_v = 1.0 / (1.0 + square)
        for chunk in range(chunks):
            for row in range(rows):
                p = chunk * rows + row
                hx, hy, hz = [h_refs[chunk][row, f, parity] for f in range(3)]
                members = (
                    times_i(kz * hx - kx * hz) * damp_g,
                    -times_i(kx * hx + kz * hz) * damp_v,
                    -square * hy * damp_v,
                )
                for t, member in enumerate(members):
                    at = (t * count + p) * 16 + parity * 8
                    terms[at : at + 8, :] = member
    for parity in range(2):
        for half in range(8):
            high, low = split(terms[pl.ds(parity * 8 + half, padded, stride=16), :])
            stacked = jnp.concatenate([high, low, high], axis=0)
            result = lax.dot_general(
                stacked, w_ref[...], (((0,), (0,)), ((), ())), preferred_element_type=F32
            )
            for part in range(2):
                for odd in range(2):
                    start = part * 1024 + odd * 16 + 2 * half + parity
                    at = part * 64 + odd * 32
                    for j in range(4):
                        sums[j][pl.ds(start, 32, stride=32), :] = result[
                            at : at + 32, j * LANES : (j + 1) * LANES
                        ]
    shape = vort_ref.shape[:3] + (LANES,)
    for j in range(2):
        lanes = pl.ds(j * LANES, LANES)
        vort_ref[:, :, :, lanes] = sums[j][...].reshape(shape)
        lapv_ref[:, :, :, lanes] = sums[2 + j][...].reshape(shape)


def exchange_kernel(*refs, jobs, sizes):
    count = len(jobs)
    sources, dests = refs[:count], refs[count : 2 * count]
    send_sem, recv_sem, local_sem = refs[2 * count :]
    position = {axis: lax.axis_index(axis) for axis in ("row", "col")}
    axes = sorted({axis for axis, _ in jobs})
    barrier = pltpu.get_barrier_semaphore()

    def target(axis, offset):
        return lax.rem(position[axis] + offset, sizes[axis])

    def device(axis, index):
        return (index, position["col"]) if axis == "row" else (position["row"], index)

    total = 0
    for axis in axes:
        for offset in range(1, sizes[axis]):
            total += 1
            pl.semaphore_signal(
                barrier,
                inc=1,
                device_id=device(axis, target(axis, offset)),
                device_id_type=MESH,
            )
    pl.semaphore_wait(barrier, total)

    def block(ref, axis, chunk, index):
        return ref.at[index] if chunk is None else ref.at[:, chunk * sizes[axis] + index]

    copies = []
    slot = 0
    for job, (axis, chunk) in enumerate(jobs):
        me = position[axis]
        for offset in range(1, sizes[axis]):
            peer = target(axis, offset)
            copy = pltpu.make_async_remote_copy(
                src_ref=block(sources[job], axis, chunk, peer),
                dst_ref=dests[job].at[me],
                send_sem=send_sem.at[slot],
                recv_sem=recv_sem.at[slot],
                device_id=device(axis, peer),
                device_id_type=MESH,
            )
            copy.start()
            copies.append(copy)
            slot += 1
    for job, (axis, chunk) in enumerate(jobs):
        me = position[axis]
        own = pltpu.make_async_copy(
            block(sources[job], axis, chunk, me), dests[job].at[me], local_sem.at[job]
        )
        own.start()
        copies.append(own)
    for copy in copies:
        copy.wait()


def exchange(jobs, arrays, sizes, collective_id):
    shapes = []
    for (axis, chunk), array in zip(jobs, arrays):
        shape = array.shape
        if chunk is not None:
            shape = (sizes[axis], shape[0]) + shape[2:]
        shapes.append(jax.ShapeDtypeStruct(shape, array.dtype))
    slots = sum(sizes[axis] - 1 for axis, _ in jobs)
    anywhere = pl.BlockSpec(memory_space=pl.ANY)
    return pl.pallas_call(
        functools.partial(exchange_kernel, jobs=tuple(jobs), sizes=sizes),
        out_shape=shapes,
        in_specs=[anywhere] * len(jobs),
        out_specs=[anywhere] * len(jobs),
        scratch_shapes=[
            pltpu.SemaphoreType.DMA((slots,)),
            pltpu.SemaphoreType.DMA((slots,)),
            pltpu.SemaphoreType.DMA((len(jobs),)),
        ],
        compiler_params=pltpu.CompilerParams(collective_id=collective_id, has_side_effects=True),
        name="exchange_%d" % collective_id,
    )(*arrays)


def rounded_halves(w):
    high = lax.reduce_precision(w, 8, 7)
    return high.astype(BF16), (w - high).astype(BF16)


def pad_rows(w, rows):
    return jnp.pad(w, ((0, rows - w.shape[0]), (0, 0)))


def params(**extra):
    return pltpu.CompilerParams(vmem_limit_bytes=VMEM_LIMIT, **extra)


def whole(shape):
    return pl.BlockSpec(shape, lambda *_: (0,) * len(shape))


def per_device_fast(v_coef, vort_coef, plane_ops, inverse_ops, sizes):
    rows, cols = sizes["row"], sizes["col"]
    _, stream_local, span_local, coefs = v_coef.shape
    count = plane_ops.shape[1]
    chunks = count // rows
    half = span_local // 2
    modes = rows * half
    stream_total, span_total = stream_local * cols, span_local * rows
    points = 3 * span_total // 2
    step = points // (2 * cols)
    stream_points = 3 * stream_total

    lane = jnp.arange(LANES, dtype=jnp.int32)
    mode = 2 * (lane % 32) + (lane // 32) % 2 + stream_local * lax.axis_index("col")
    kx = (STREAM_STEP * mode.astype(F32))[None, :]
    signed = signed_order(rows, span_local, span_total)
    kz_all = np.broadcast_to(
        (np.float32(SPAN_STEP) * signed.astype(np.float32))[..., None], signed.shape + (LANES,)
    )
    n_here = (
        span_local * lax.axis_index("row")
        + jnp.arange(2, dtype=jnp.int32)[:, None]
        + 2 * jnp.arange(half, dtype=jnp.int32)[None, :]
    )
    signed_here = jnp.where(n_here < span_total // 2, n_here, n_here - span_total)
    kz_here = jnp.broadcast_to(
        (SPAN_STEP * signed_here.astype(F32))[..., None], (2, half, LANES)
    )
    span_in, span_out = span_fast_tables(rows, span_local, span_total)
    stream_in, stream_out = stream_fast_tables(stream_total)

    weights = []
    for ops, rows_used in ((plane_ops, 3), (plane_ops[:2], 2)):
        flat = ops.reshape(rows_used * count, coefs)
        padded = -(-rows_used * count // 16) * 16
        weights.append(jnp.concatenate([pad_rows(w, padded) for w in rounded_halves(flat)], axis=0))

    coef_spec = [
        pl.BlockSpec((2, stream_local, 16, LANES), lambda i: (0, 0, i, 0)),
        pl.BlockSpec((2, stream_local, 16, LANES), lambda i: (0, 0, i, 1)),
    ]
    values = pl.pallas_call(
        functools.partial(plane_kernel, count=count),
        grid=(span_local // 16,),
        out_shape=jax.ShapeDtypeStruct((5 * count, 2, half, LANES), F32),
        in_specs=coef_spec + coef_spec + [whole(w.shape) for w in weights],
        out_specs=pl.BlockSpec((5 * count, 2, 8, LANES), lambda i: (0, 0, i, 0)),
        compiler_params=params(),
        name="plane_values",
    )(v_coef, v_coef, vort_coef, vort_coef, *weights)
    values = values.reshape(5, count, 2, half, LANES)

    def span_inverse(received):
        return pl.pallas_call(
            functools.partial(span_inverse_kernel, rows=rows, half=half),
            grid=(3,),
            out_shape=jax.ShapeDtypeStruct((cols, 6, 2 * step, LANES), F32),
            in_specs=[
                whole((rows, 5, 2, half, LANES)),
                whole((1, LANES)),
                whole(kz_all.shape),
                whole(span_in.shape),
            ],
            out_specs=pl.BlockSpec((cols, 2, 2 * step, LANES), lambda i: (0, i, 0, 0)),
            scratch_shapes=[pltpu.VMEM((3, 2, 2 * modes, 2 * LANES), BF16)] * 2,
            compiler_params=params(),
            name="span_inverse",
        )(received, kx, jnp.asarray(kz_all), jnp.asarray(span_in))

    def stream_products(arrived):
        block = 48
        return pl.pallas_call(
            stream_kernel,
            grid=(2 * step // block,),
            out_shape=jax.ShapeDtypeStruct((cols, 3, 2 * step, LANES), F32),
            in_specs=[
                pl.BlockSpec((cols, 6, block, LANES), lambda i: (0, 0, i, 0)),
                whole(stream_in.shape),
                whole(stream_out.shape),
            ],
            out_specs=pl.BlockSpec((cols, 3, block, LANES), lambda i: (0, 0, i, 0)),
            compiler_params=params(),
            name="stream_products",
        )(arrived, jnp.asarray(stream_in), jnp.asarray(stream_out))

    def span_forward(returned):
        return pl.pallas_call(
            span_forward_kernel,
            out_shape=jax.ShapeDtypeStruct((rows, 3, 2, half, LANES), F32),
            compiler_params=params(),
            name="span_forward",
        )(returned, jnp.asarray(span_out))

    state = [values] * chunks
    after = [span_inverse, stream_products, span_forward, lambda home: home]
    axes = ["row", "col", "col", "row"]
    for turn in range(chunks + 3):
        active = [c for c in range(chunks) if 0 <= turn - c < 4]
        jobs = [(axes[turn - c], c if turn == c else None) for c in active]
        results = exchange(jobs, [state[c] for c in active], sizes, turn)
        for c, result in zip(active, results):
            state[c] = after[turn - c](result)

    inv0, inv1 = inverse_ops[0].T, inverse_ops[1].T
    none = jnp.zeros_like(inv0)
    table = jnp.concatenate(
        [
            jnp.concatenate([inv0, none], axis=1),
            jnp.concatenate([none, inv1], axis=1),
            jnp.concatenate([none, inv0], axis=1),
        ],
        axis=0,
    )
    padded = -(-3 * count // 16) * 16
    high, low = [pad_rows(w, padded) for w in rounded_halves(table)]
    table = jnp.concatenate([high, high, low], axis=0)
    out_block = pl.BlockSpec((2, stream_local, 16, coefs), lambda i: (0, 0, i, 0))
    return pl.pallas_call(
        functools.partial(combine_kernel, chunks=chunks, rows=rows, count=count),
        grid=(span_local // 16,),
        out_shape=[jax.ShapeDtypeStruct(v_coef.shape, F32)] * 2,
        in_specs=[pl.BlockSpec((rows, 3, 2, 8, LANES), lambda i: (0, 0, 0, i, 0))] * chunks
        + [
            whole((1, LANES)),
            pl.BlockSpec((2, 8, LANES), lambda i: (0, i, 0)),
            whole(table.shape),
        ],
        out_specs=[out_block] * 2,
        scratch_shapes=[pltpu.VMEM((padded * 16, LANES), F32)]
        + [pltpu.VMEM((2 * stream_local * 16, LANES), F32)] * 4,
        compiler_params=params(),
        name="combinations",
    )(*state, kx, kz_here, table)


def signed_modes(first, count, total):
    modes = first + jnp.arange(count, dtype=jnp.int32)
    return jnp.where(modes < total // 2, modes, modes - total)


def span_tables(total):
    points = 3 * total // 2
    n = np.arange(total)
    signed = np.where(n < total // 2, n, n - total)
    angle = np.mod(signed[:, None] * np.arange(points)[None, :], points) * (2.0 * math.pi / points)
    cosine, sine = np.cos(angle), np.sin(angle)
    inverse = np.stack(
        [np.stack([cosine, sine], axis=1), np.stack([-sine, cosine], axis=1)], axis=0
    )
    forward = np.stack(
        [np.stack([cosine.T, -sine.T], axis=1), np.stack([sine.T, cosine.T], axis=1)], axis=0
    ) * (FORWARD_SCALE / points)
    return jnp.asarray(inverse, F32), jnp.asarray(forward, F32)


def stream_tables(total):
    points = 3 * total
    modes = np.arange(total)
    angle = np.mod(modes[:, None] * np.arange(points)[None, :], points) * (2.0 * math.pi / points)
    cosine, sine = np.cos(angle), np.sin(angle)
    weights = np.where(modes == 0, 1.0, 2.0)[:, None]
    inverse = np.stack([weights * cosine, -weights * sine], axis=0) * INVERSE_SCALE
    forward = np.stack([cosine.T, -sine.T], axis=1) / points
    return jnp.asarray(inverse, F32), jnp.asarray(forward, F32)


def rotate(pair, factor):
    return (-factor * pair[1], factor * pair[0])


def combine(first, second, sign):
    return (first[0] + sign * second[0], first[1] + sign * second[1])


def scaled(pair, factor):
    return (pair[0] * factor, pair[1] * factor)


def split_pair(values):
    return (values[..., 0, :], values[..., 1, :])


def join_pair(pair):
    return jnp.stack(pair, axis=-2)


def build_fields(values, stream, span):
    v_base = split_pair(values[0])
    v_slope = split_pair(values[1])
    v_curve = split_pair(values[2])
    g_base = split_pair(values[3])
    g_slope = split_pair(values[4])
    square = stream * stream + span * span
    recip = 1.0 / jnp.where(square > 0, square, 1.0)
    along = scaled(combine(rotate(v_slope, stream), rotate(g_base, span), -1.0), recip)
    across = scaled(combine(rotate(v_slope, span), rotate(g_base, stream), 1.0), recip)
    omega_x = combine(
        scaled(combine(rotate(v_curve, span), rotate(g_slope, stream), 1.0), recip),
        rotate(v_base, span),
        -1.0,
    )
    omega_z = combine(
        rotate(v_base, stream),
        scaled(combine(rotate(v_curve, stream), rotate(g_slope, span), -1.0), recip),
        -1.0,
    )
    group_members = [along, v_base, across, omega_x, g_base, omega_z]
    return jnp.stack([join_pair(member) for member in group_members], axis=0)


def per_device(v_coef, vort_coef, plane_ops, inverse_ops):
    row_count = lax.axis_size("row")
    column_total_count = lax.axis_size("col")
    stream_local = v_coef.shape[1]
    span_local = v_coef.shape[2]
    stream_total = stream_local * column_total_count
    span_total = span_local * row_count
    stream_first = lax.axis_index("col") * stream_local
    span_first = lax.axis_index("row") * span_local
    stream_here = (
        STREAM_STEP * (stream_first + jnp.arange(stream_local, dtype=jnp.int32)).astype(jnp.float32)
    )[:, None]
    span_here = (SPAN_STEP * signed_modes(span_first, span_local, span_total).astype(jnp.float32))[
        None, :
    ]
    span_in, span_out = span_tables(span_total)
    stream_in, stream_out = stream_tables(stream_total)
    v_values = jnp.einsum("rpj,cxkj->rpxck", plane_ops, v_coef, precision=PRECISE)
    g_values = jnp.einsum("rpj,cxkj->rpxck", plane_ops[:2], vort_coef, precision=PRECISE)
    values = jnp.concatenate([v_values, g_values], axis=0)
    fields = build_fields(values, stream_here, span_here)
    pencils = lax.all_to_all(fields, "row", split_axis=1, concat_axis=4, tiled=True)
    span_phys = jnp.einsum("fpxck,ckdz->fpdxz", pencils, span_in, precision=PRECISE)
    arrived = lax.all_to_all(span_phys, "col", split_axis=4, concat_axis=3, tiled=True)
    physical = jnp.einsum("fpcmz,cmx->fpzx", arrived, stream_in, precision=PRECISE)
    velocity = physical[0:3]
    vorticity = physical[3:6]
    product_streamwise = velocity[1] * vorticity[2] - velocity[2] * vorticity[1]
    product_normal = velocity[2] * vorticity[0] - velocity[0] * vorticity[2]
    product_spanwise = velocity[0] * vorticity[1] - velocity[1] * vorticity[0]
    products = jnp.stack([product_streamwise, product_normal, product_spanwise], axis=0)
    stream_spec = jnp.einsum("fpzx,xcm->fpcmz", products, stream_out, precision=PRECISE)
    returned = lax.all_to_all(stream_spec, "col", split_axis=3, concat_axis=4, tiled=True)
    full_spec = jnp.einsum("fpdxz,dzck->fpxck", returned, span_out, precision=PRECISE)
    home = lax.all_to_all(full_spec, "row", split_axis=4, concat_axis=1, tiled=True)
    h_x = split_pair(home[0])
    h_y = split_pair(home[1])
    h_z = split_pair(home[2])
    square = stream_here * stream_here + span_here * span_here
    g_term = combine(rotate(h_x, span_here), rotate(h_z, stream_here), -1.0)
    s_term = scaled(combine(rotate(h_x, stream_here), rotate(h_z, span_here), 1.0), -1.0)
    y_term = scaled(h_y, -square)
    damp_g = 1.0 / jnp.sqrt(1.0 + square)
    damp_v = 1.0 / (1.0 + square)

    def contract(matrix, term):
        return jnp.einsum("jp,pxck->cxkj", matrix, join_pair(term), precision=PRECISE)

    vort_rhs = contract(inverse_ops[0], g_term) * damp_g[None, :, :, None]
    lapv_sum = contract(inverse_ops[1], s_term) + contract(inverse_ops[0], y_term)
    lapv_rhs = lapv_sum * damp_v[None, :, :, None]
    return (vort_rhs, lapv_rhs)


def solution(mesh):
    in_specs = (P(None, "col", "row", None), P(None, "col", "row", None), P(), P())
    out_specs = (P(None, "col", "row", None), P(None, "col", "row", None))
    sizes = {"row": mesh.shape["row"], "col": mesh.shape["col"]}

    def choose(v_coef, vort_coef, plane_ops, inverse_ops):
        args = (v_coef, vort_coef, plane_ops, inverse_ops)
        fits = (
            2 * v_coef.shape[1] == LANES
            and v_coef.shape[2] % 32 == 0
            and v_coef.shape[3] == 2 * LANES
            and plane_ops.shape[1] % sizes["row"] == 0
            and sizes["col"] == 8
        )
        return per_device_fast(*args, sizes) if fits else per_device(*args)

    return jax.shard_map(choose, mesh=mesh, in_specs=in_specs, out_specs=out_specs, check_vma=False)
```

```python
import functools
import math

import jax
import jax.numpy as jnp
import ml_dtypes
import numpy as np
from jax import lax
from jax.experimental import pallas as pl
from jax.experimental.pallas import tpu as pltpu
from jax.sharding import PartitionSpec as P

PRECISE = lax.Precision.HIGHEST
STREAM_STEP = 0.25
SPAN_STEP = 2.0 / 3.0
INVERSE_SCALE = 1.0 / 32.0
FORWARD_SCALE = 32.0
LANES = 128
VMEM_LIMIT = 44 * 1024 * 1024
MESH = pl.DeviceIdType.MESH
F32 = jnp.float32
BF16 = jnp.bfloat16


def halves(table):
    table = np.asarray(table, np.float32)
    high = table.astype(ml_dtypes.bfloat16)
    low = (table - high.astype(np.float32)).astype(ml_dtypes.bfloat16)
    return np.stack([high, low], axis=0)


def signed_order(rows, span_local, span_total):
    n = (
        span_local * np.arange(rows)[:, None, None]
        + np.arange(2)[None, :, None]
        + 2 * np.arange(span_local // 2)[None, None, :]
    )
    return np.where(n < span_total // 2, n, n - span_total)


def span_fast_tables(rows, span_local, span_total):
    points = 3 * span_total // 2
    signed = signed_order(rows, span_local, span_total)
    grid = np.arange(points // 2)
    inverse, forward = [], []
    for parity in range(2):
        s = signed[:, parity, :].reshape(-1)
        angle = np.mod(s[None, :] * grid[:, None], points) * (2.0 * math.pi / points)
        inverse.append(np.concatenate([np.cos(angle), np.sin(angle)], axis=1))
        factor = FORWARD_SCALE / points
        forward.append(np.concatenate([np.cos(angle).T, np.sin(angle).T], axis=1) * factor)
    return halves(np.stack(inverse)), halves(np.stack(forward))


def stream_fast_tables(total):
    points = 3 * total
    grid = np.arange(points // 4) + 0.5
    inverse, forward = [], []
    for part in range(2):
        for parity in range(2):
            m = 2 * np.arange(total // 2) + parity
            angle = np.mod(m[:, None] * grid[None, :], points) * (2.0 * math.pi / points)
            wave = np.cos(angle) if part == 0 else -np.sin(angle)
            weight = np.where(m == 0, 1.0, 2.0)[:, None]
            inverse.append(weight * wave * INVERSE_SCALE)
            forward.append(wave.T / points)
    return halves(np.stack(inverse)), halves(np.stack(forward))


def split(values):
    high = values.astype(BF16)
    return high, (values - high.astype(F32)).astype(BF16)


def dot(a, b):
    return jnp.dot(a, b, preferred_element_type=F32)


def dot3(a_high, a_low, b_high, b_low):
    return dot(a_high, b_high) + (dot(a_high, b_low) + dot(a_low, b_high))


def times_i(values):
    axis = values.ndim - 1
    lane = lax.broadcasted_iota(jnp.int32, values.shape, axis)
    turned = pltpu.roll(values, LANES // 2, axis)
    return jnp.where(lane < LANES // 2, -turned, turned)


def block_transpose(a):
    lane = lax.broadcasted_iota(jnp.int32, a[0].shape, 1)
    left = lane < 64
    odd = (lane // 32) % 2 == 1
    t = [None] * 4
    for s in range(2):
        t[s] = jnp.where(left, a[s], pltpu.roll(a[s + 2], 64, 1))
        t[s + 2] = jnp.where(left, pltpu.roll(a[s], 64, 1), a[s + 2])
    out = [None] * 4
    for s in (0, 2):
        out[s] = jnp.where(odd, pltpu.roll(t[s + 1], 32, 1), t[s])
        out[s + 1] = jnp.where(odd, t[s + 1], pltpu.roll(t[s], 96, 1))
    return out


def contract_last(a, b):
    return lax.dot_general(a, b, (((1,), (1,)), ((), ())), preferred_element_type=F32)


def plane_kernel(v_ref, g_ref, first_ref, second_ref, out_ref, y_ref):
    used = out_ref.shape[0]
    flat = out_ref.reshape(used * 16, LANES)
    for part in range(2):
        for side in range(2):
            at = pl.ds(side * 32, 32)
            rows = [ref[part, at].reshape(512, 2 * LANES) for ref in (v_ref, g_ref)]
            high, low = split(jnp.concatenate(rows, axis=1))
            y = dot(high, first_ref[...])
            y = y + pltpu.roll(y, LANES // 2, 1) + dot(low, second_ref[...])
            y_ref[pl.ds((2 * part + side) * 512, 512), :] = y
    for parity in range(2):
        for half in range(8):
            rows = []
            for part in range(2):
                for odd in range(2):
                    start = part * 1024 + odd * 16 + 2 * half + parity
                    rows.append(y_ref[pl.ds(start, 32, stride=32), :])
            turned = jnp.concatenate(rows, axis=0).T
            flat[pl.ds(parity * 8 + half, used, stride=16), :] = turned[:used]


def span_inverse_kernel(r_ref, kx_ref, kz_ref, t_ref, out_ref, high_ref, low_ref, *, rows, half):
    modes = rows * half

    @pl.when(pl.program_id(0) == 0)
    def _():
        kx = kx_ref[...]
        for row in range(rows):
            for parity in range(2):
                kz = kz_ref[row, parity]
                square = kx * kx + kz * kz
                recip = 1.0 / jnp.where(square > 0, square, 1.0)
                vb, vd, vdd, gb, gd = [r_ref[row, f, parity] for f in range(5)]
                members = [
                    times_i((kx * vd - kz * gb) * recip),
                    vb,
                    times_i((kz * vd + kx * gb) * recip),
                    times_i((kz * vdd + kx * gd) * recip - kz * vb),
                    gb,
                    times_i(kx * vb - (kx * vdd - kz * gd) * recip),
                ]
                for f, member in enumerate(members):
                    for place, values in ((0, member), (modes, times_i(member))):
                        high, low = split(values)
                        at = pl.ds(place + row * half, half)
                        high_ref[f // 2, parity, at, pl.ds((f % 2) * LANES, LANES)] = high
                        low_ref[f // 2, parity, at, pl.ds((f % 2) * LANES, LANES)] = low

    pair = pl.program_id(0)
    even, odd = [
        dot3(t_ref[0, q], t_ref[1, q], high_ref[pair, q], low_ref[pair, q]) for q in range(2)
    ]
    plus, minus = even + odd, even - odd
    dests = out_ref.shape[0]
    step = out_ref.shape[2] // 2
    for d in range(dests):
        for f in range(2):
            lanes = slice(f * LANES, (f + 1) * LANES)
            out_ref[d, f, :step] = plus[d * step : (d + 1) * step, lanes]
            out_ref[d, f, step:] = minus[d * step : (d + 1) * step, lanes]


def stream_kernel(x_ref, ti_ref, tf_ref, out_ref):
    sources, fields, block, _ = x_ref.shape
    width = ti_ref.shape[3]
    parts = [x_ref[s].reshape(fields * block, LANES) for s in range(sources)]
    groups = [[] for _ in range(4)]
    for s in range(0, sources, 4):
        for g, piece in enumerate(block_transpose(parts[s : s + 4])):
            groups[g].append(piece)
    spectral = []
    for g in range(4):
        high, low = split(jnp.concatenate(groups[g], axis=1))
        spectral.append(dot3(high, low, ti_ref[0, g], ti_ref[1, g]))
    ce, co, se, so = [s.reshape(fields, block, width) for s in spectral]
    a, b, c, d = ce + co, se + so, ce - co, se - so
    products = []
    for image in (a + b, a - b, c + d, c - d):
        u, v, w, ox, oy, oz = [image[f] for f in range(6)]
        products.append(jnp.stack([v * oz - w * oy, w * ox - u * oz, u * oy - v * ox], axis=0))
    h1, h2, h3, h4 = [h.reshape(3 * block, width) for h in products]
    sum1, sum2, dif1, dif2 = h1 + h2, h3 + h4, h1 - h2, h3 - h4
    results = []
    for g, h in enumerate((sum1 + sum2, sum1 - sum2, dif1 + dif2, dif1 - dif2)):
        high, low = split(h)
        results.append(dot3(high, low, tf_ref[0, g], tf_ref[1, g]))
    for s in range(0, sources, 4):
        at = (s // 4) * LANES
        pieces = block_transpose([r[:, at : at + LANES] for r in results])
        for k in range(4):
            out_ref[s + k] = pieces[k].reshape(3, block, LANES)


def span_forward_kernel(x_ref, t_ref, out_ref):
    sources, fields, both, _ = x_ref.shape
    step = both // 2
    rows, half = out_ref.shape[0], out_ref.shape[3]
    for parity in range(2):
        columns = []
        for f in range(fields):
            first, second = x_ref[:, f, :step], x_ref[:, f, step:]
            h = first + second if parity == 0 else first - second
            h = h.reshape(sources * step, LANES)
            columns.append(jnp.concatenate([h, -times_i(h)], axis=0))
        high, low = split(jnp.concatenate(columns, axis=1))
        result = dot3(t_ref[0, parity], t_ref[1, parity], high, low)
        for row in range(rows):
            for f in range(fields):
                out_ref[row, f, parity] = result[
                    row * half : (row + 1) * half, f * LANES : (f + 1) * LANES
                ]


def combine_kernel(*refs, chunks, rows, count):
    h_refs = refs[:chunks]
    kx_ref, kz_ref, w_ref, vort_ref, lapv_ref, terms, left = refs[chunks:]
    kx = kx_ref[...]
    padded = terms.shape[0] // 16
    if padded > 3 * count:
        terms[3 * count * 16 :, :] = jnp.zeros(((padded - 3 * count) * 16, LANES), F32)
    for parity in range(2):
        kz = kz_ref[parity]
        square = kx * kx + kz * kz
        damp_g = 1.0 / jnp.sqrt(1.0 + square)
        damp_v = 1.0 / (1.0 + square)
        for chunk in range(chunks):
            for row in range(rows):
                p = chunk * rows + row
                hx, hy, hz = [h_refs[chunk][row, f, parity] for f in range(3)]
                members = (
                    times_i(kz * hx - kx * hz) * damp_g,
                    -times_i(kx * hx + kz * hz) * damp_v,
                    -square * hy * damp_v,
                )
                for t, member in enumerate(members):
                    at = (t * count + p) * 16 + parity * 8
                    terms[at : at + 8, :] = member
    for parity in range(2):
        for half in range(8):
            values = terms[pl.ds(parity * 8 + half, padded, stride=16), :]
            high = values.astype(BF16).astype(F32)
            rest = jnp.zeros((LANES - 3 * padded, LANES), F32)
            turned = jnp.concatenate([high, values - high, high, rest], axis=0).T
            for part in range(2):
                for odd in range(2):
                    start = part * 1024 + odd * 16 + 2 * half + parity
                    at = part * 64 + odd * 32
                    left[pl.ds(start, 32, stride=32), :] = turned[at : at + 32]
    for part in range(2):
        for side in range(2):
            rows = left[pl.ds((2 * part + side) * 512, 512), :].astype(BF16)
            result = dot(rows, w_ref[...]).reshape(32, 16, 4 * LANES)
            vort_ref[part, pl.ds(side * 32, 32)] = result[:, :, : 2 * LANES]
            lapv_ref[part, pl.ds(side * 32, 32)] = result[:, :, 2 * LANES :]


def exchange_kernel(*refs, jobs, sizes):
    count = len(jobs)
    sources, dests = refs[:count], refs[count : 2 * count]
    send_sem, recv_sem, local_sem = refs[2 * count :]
    position = {axis: lax.axis_index(axis) for axis in ("row", "col")}
    axes = sorted({axis for axis, _ in jobs})
    barrier = pltpu.get_barrier_semaphore()

    def target(axis, offset):
        return lax.rem(position[axis] + offset, sizes[axis])

    def device(axis, index):
        return (index, position["col"]) if axis == "row" else (position["row"], index)

    total = 0
    for axis in axes:
        for offset in range(1, sizes[axis]):
            total += 1
            pl.semaphore_signal(
                barrier,
                inc=1,
                device_id=device(axis, target(axis, offset)),
                device_id_type=MESH,
            )
    pl.semaphore_wait(barrier, total)

    def block(ref, axis, chunk, index):
        return ref.at[index] if chunk is None else ref.at[:, chunk * sizes[axis] + index]

    copies = []
    slot = 0
    for job, (axis, chunk) in enumerate(jobs):
        me = position[axis]
        for offset in range(1, sizes[axis]):
            peer = target(axis, offset)
            copy = pltpu.make_async_remote_copy(
                src_ref=block(sources[job], axis, chunk, peer),
                dst_ref=dests[job].at[me],
                send_sem=send_sem.at[slot],
                recv_sem=recv_sem.at[slot],
                device_id=device(axis, peer),
                device_id_type=MESH,
            )
            copy.start()
            copies.append(copy)
            slot += 1
    for job, (axis, chunk) in enumerate(jobs):
        me = position[axis]
        own = pltpu.make_async_copy(
            block(sources[job], axis, chunk, me), dests[job].at[me], local_sem.at[job]
        )
        own.start()
        copies.append(own)
    for copy in copies:
        copy.wait()


def exchange(jobs, arrays, sizes, collective_id):
    shapes = []
    for (axis, chunk), array in zip(jobs, arrays):
        shape = array.shape
        if chunk is not None:
            shape = (sizes[axis], shape[0]) + shape[2:]
        shapes.append(jax.ShapeDtypeStruct(shape, array.dtype))
    slots = sum(sizes[axis] - 1 for axis, _ in jobs)
    anywhere = pl.BlockSpec(memory_space=pl.ANY)
    return pl.pallas_call(
        functools.partial(exchange_kernel, jobs=tuple(jobs), sizes=sizes),
        out_shape=shapes,
        in_specs=[anywhere] * len(jobs),
        out_specs=[anywhere] * len(jobs),
        scratch_shapes=[
            pltpu.SemaphoreType.DMA((slots,)),
            pltpu.SemaphoreType.DMA((slots,)),
            pltpu.SemaphoreType.DMA((len(jobs),)),
        ],
        compiler_params=pltpu.CompilerParams(collective_id=collective_id, has_side_effects=True),
        name="exchange_%d" % collective_id,
    )(*arrays)


def rounded_halves(w):
    high = lax.reduce_precision(w, 8, 7)
    return high.astype(BF16), (w - high).astype(BF16)


def pad_rows(w, rows):
    return jnp.pad(w, ((0, rows - w.shape[0]), (0, 0)))


def params(**extra):
    return pltpu.CompilerParams(vmem_limit_bytes=VMEM_LIMIT, **extra)


def whole(shape):
    return pl.BlockSpec(shape, lambda *_: (0,) * len(shape))


def per_device_fast(v_coef, vort_coef, plane_ops, inverse_ops, sizes):
    rows, cols = sizes["row"], sizes["col"]
    _, stream_local, span_local, coefs = v_coef.shape
    count = plane_ops.shape[1]
    chunks = count // rows
    half = span_local // 2
    modes = rows * half
    stream_total, span_total = stream_local * cols, span_local * rows
    points = 3 * span_total // 2
    step = points // (2 * cols)
    stream_points = 3 * stream_total

    lane = jnp.arange(LANES, dtype=jnp.int32)
    mode = 2 * (lane % 32) + (lane // 32) % 2 + stream_local * lax.axis_index("col")
    kx = (STREAM_STEP * mode.astype(F32))[None, :]
    signed = signed_order(rows, span_local, span_total)
    kz_all = np.broadcast_to(
        (np.float32(SPAN_STEP) * signed.astype(np.float32))[..., None], signed.shape + (LANES,)
    )
    n_here = (
        span_local * lax.axis_index("row")
        + jnp.arange(2, dtype=jnp.int32)[:, None]
        + 2 * jnp.arange(half, dtype=jnp.int32)[None, :]
    )
    signed_here = jnp.where(n_here < span_total // 2, n_here, n_here - span_total)
    kz_here = jnp.broadcast_to(
        (SPAN_STEP * signed_here.astype(F32))[..., None], (2, half, LANES)
    )
    span_in, span_out = span_fast_tables(rows, span_local, span_total)
    stream_in, stream_out = stream_fast_tables(stream_total)

    used = 5 * count
    highs, lows = [], []
    for ops, before, after in ((plane_ops, 0, 2), (plane_ops[:2], 3, 0)):
        flat = ops.reshape(-1, coefs).T
        for kept, w in zip((highs, lows), rounded_halves(flat)):
            kept.append(jnp.pad(w, ((0, 0), (before * count, after * count + 64 - used))))
    high, low = [jnp.concatenate(kept, axis=0) for kept in (highs, lows)]
    weights = [
        jnp.concatenate([high, low], axis=1),
        jnp.concatenate([high, jnp.zeros_like(high)], axis=1),
    ]

    coef_spec = pl.BlockSpec((2, stream_local, 16, coefs), lambda i: (0, 0, i, 0))
    values = pl.pallas_call(
        plane_kernel,
        grid=(span_local // 16,),
        out_shape=jax.ShapeDtypeStruct((5 * count, 2, half, LANES), F32),
        in_specs=[coef_spec] * 2 + [whole(w.shape) for w in weights],
        out_specs=pl.BlockSpec((5 * count, 2, 8, LANES), lambda i: (0, 0, i, 0)),
        scratch_shapes=[pltpu.VMEM((2 * stream_local * 16, LANES), F32)],
        compiler_params=params(),
        name="plane_values",
    )(v_coef, vort_coef, *weights)
    values = values.reshape(5, count, 2, half, LANES)

    def span_inverse(received):
        return pl.pallas_call(
            functools.partial(span_inverse_kernel, rows=rows, half=half),
            grid=(3,),
            out_shape=jax.ShapeDtypeStruct((cols, 6, 2 * step, LANES), F32),
            in_specs=[
                whole((rows, 5, 2, half, LANES)),
                whole((1, LANES)),
                whole(kz_all.shape),
                whole(span_in.shape),
            ],
            out_specs=pl.BlockSpec((cols, 2, 2 * step, LANES), lambda i: (0, i, 0, 0)),
            scratch_shapes=[pltpu.VMEM((3, 2, 2 * modes, 2 * LANES), BF16)] * 2,
            compiler_params=params(),
            name="span_inverse",
        )(received, kx, jnp.asarray(kz_all), jnp.asarray(span_in))

    def stream_products(arrived):
        block = 48
        return pl.pallas_call(
            stream_kernel,
            grid=(2 * step // block,),
            out_shape=jax.ShapeDtypeStruct((cols, 3, 2 * step, LANES), F32),
            in_specs=[
                pl.BlockSpec((cols, 6, block, LANES), lambda i: (0, 0, i, 0)),
                whole(stream_in.shape),
                whole(stream_out.shape),
            ],
            out_specs=pl.BlockSpec((cols, 3, block, LANES), lambda i: (0, 0, i, 0)),
            compiler_params=params(),
            name="stream_products",
        )(arrived, jnp.asarray(stream_in), jnp.asarray(stream_out))

    def span_forward(returned):
        return pl.pallas_call(
            span_forward_kernel,
            out_shape=jax.ShapeDtypeStruct((rows, 3, 2, half, LANES), F32),
            compiler_params=params(),
            name="span_forward",
        )(returned, jnp.asarray(span_out))

    state = [values] * chunks
    after = [span_inverse, stream_products, span_forward, lambda home: home]
    axes = ["row", "col", "col", "row"]
    for turn in range(chunks + 3):
        active = [c for c in range(chunks) if 0 <= turn - c < 4]
        jobs = [(axes[turn - c], c if turn == c else None) for c in active]
        results = exchange(jobs, [state[c] for c in active], sizes, turn)
        for c, result in zip(active, results):
            state[c] = after[turn - c](result)

    inv0, inv1 = inverse_ops[0].T, inverse_ops[1].T
    none = jnp.zeros_like(inv0)
    table = jnp.concatenate(
        [
            jnp.concatenate([inv0, none], axis=1),
            jnp.concatenate([none, inv1], axis=1),
            jnp.concatenate([none, inv0], axis=1),
        ],
        axis=0,
    )
    padded = -(-3 * count // 8) * 8
    high, low = [pad_rows(w, padded) for w in rounded_halves(table)]
    table = pad_rows(jnp.concatenate([high, high, low], axis=0), LANES)
    out_block = pl.BlockSpec((2, stream_local, 16, coefs), lambda i: (0, 0, i, 0))
    return pl.pallas_call(
        functools.partial(combine_kernel, chunks=chunks, rows=rows, count=count),
        grid=(span_local // 16,),
        out_shape=[jax.ShapeDtypeStruct(v_coef.shape, F32)] * 2,
        in_specs=[pl.BlockSpec((rows, 3, 2, 8, LANES), lambda i: (0, 0, 0, i, 0))] * chunks
        + [
            whole((1, LANES)),
            pl.BlockSpec((2, 8, LANES), lambda i: (0, i, 0)),
            whole(table.shape),
        ],
        out_specs=[out_block] * 2,
        scratch_shapes=[pltpu.VMEM((padded * 16, LANES), F32)]
        + [pltpu.VMEM((2 * stream_local * 16, LANES), F32)],
        compiler_params=params(),
        name="combinations",
    )(*state, kx, kz_here, table)


def signed_modes(first, count, total):
    modes = first + jnp.arange(count, dtype=jnp.int32)
    return jnp.where(modes < total // 2, modes, modes - total)


def span_tables(total):
    points = 3 * total // 2
    n = np.arange(total)
    signed = np.where(n < total // 2, n, n - total)
    angle = np.mod(signed[:, None] * np.arange(points)[None, :], points) * (2.0 * math.pi / points)
    cosine, sine = np.cos(angle), np.sin(angle)
    inverse = np.stack(
        [np.stack([cosine, sine], axis=1), np.stack([-sine, cosine], axis=1)], axis=0
    )
    forward = np.stack(
        [np.stack([cosine.T, -sine.T], axis=1), np.stack([sine.T, cosine.T], axis=1)], axis=0
    ) * (FORWARD_SCALE / points)
    return jnp.asarray(inverse, F32), jnp.asarray(forward, F32)


def stream_tables(total):
    points = 3 * total
    modes = np.arange(total)
    angle = np.mod(modes[:, None] * np.arange(points)[None, :], points) * (2.0 * math.pi / points)
    cosine, sine = np.cos(angle), np.sin(angle)
    weights = np.where(modes == 0, 1.0, 2.0)[:, None]
    inverse = np.stack([weights * cosine, -weights * sine], axis=0) * INVERSE_SCALE
    forward = np.stack([cosine.T, -sine.T], axis=1) / points
    return jnp.asarray(inverse, F32), jnp.asarray(forward, F32)


def rotate(pair, factor):
    return (-factor * pair[1], factor * pair[0])


def combine(first, second, sign):
    return (first[0] + sign * second[0], first[1] + sign * second[1])


def scaled(pair, factor):
    return (pair[0] * factor, pair[1] * factor)


def split_pair(values):
    return (values[..., 0, :], values[..., 1, :])


def join_pair(pair):
    return jnp.stack(pair, axis=-2)


def build_fields(values, stream, span):
    v_base = split_pair(values[0])
    v_slope = split_pair(values[1])
    v_curve = split_pair(values[2])
    g_base = split_pair(values[3])
    g_slope = split_pair(values[4])
    square = stream * stream + span * span
    recip = 1.0 / jnp.where(square > 0, square, 1.0)
    along = scaled(combine(rotate(v_slope, stream), rotate(g_base, span), -1.0), recip)
    across = scaled(combine(rotate(v_slope, span), rotate(g_base, stream), 1.0), recip)
    omega_x = combine(
        scaled(combine(rotate(v_curve, span), rotate(g_slope, stream), 1.0), recip),
        rotate(v_base, span),
        -1.0,
    )
    omega_z = combine(
        rotate(v_base, stream),
        scaled(combine(rotate(v_curve, stream), rotate(g_slope, span), -1.0), recip),
        -1.0,
    )
    group_members = [along, v_base, across, omega_x, g_base, omega_z]
    return jnp.stack([join_pair(member) for member in group_members], axis=0)


def per_device(v_coef, vort_coef, plane_ops, inverse_ops):
    row_count = lax.axis_size("row")
    column_total_count = lax.axis_size("col")
    stream_local = v_coef.shape[1]
    span_local = v_coef.shape[2]
    stream_total = stream_local * column_total_count
    span_total = span_local * row_count
    stream_first = lax.axis_index("col") * stream_local
    span_first = lax.axis_index("row") * span_local
    stream_here = (
        STREAM_STEP * (stream_first + jnp.arange(stream_local, dtype=jnp.int32)).astype(jnp.float32)
    )[:, None]
    span_here = (SPAN_STEP * signed_modes(span_first, span_local, span_total).astype(jnp.float32))[
        None, :
    ]
    span_in, span_out = span_tables(span_total)
    stream_in, stream_out = stream_tables(stream_total)
    v_values = jnp.einsum("rpj,cxkj->rpxck", plane_ops, v_coef, precision=PRECISE)
    g_values = jnp.einsum("rpj,cxkj->rpxck", plane_ops[:2], vort_coef, precision=PRECISE)
    values = jnp.concatenate([v_values, g_values], axis=0)
    fields = build_fields(values, stream_here, span_here)
    pencils = lax.all_to_all(fields, "row", split_axis=1, concat_axis=4, tiled=True)
    span_phys = jnp.einsum("fpxck,ckdz->fpdxz", pencils, span_in, precision=PRECISE)
    arrived = lax.all_to_all(span_phys, "col", split_axis=4, concat_axis=3, tiled=True)
    physical = jnp.einsum("fpcmz,cmx->fpzx", arrived, stream_in, precision=PRECISE)
    velocity = physical[0:3]
    vorticity = physical[3:6]
    product_streamwise = velocity[1] * vorticity[2] - velocity[2] * vorticity[1]
    product_normal = velocity[2] * vorticity[0] - velocity[0] * vorticity[2]
    product_spanwise = velocity[0] * vorticity[1] - velocity[1] * vorticity[0]
    products = jnp.stack([product_streamwise, product_normal, product_spanwise], axis=0)
    stream_spec = jnp.einsum("fpzx,xcm->fpcmz", products, stream_out, precision=PRECISE)
    returned = lax.all_to_all(stream_spec, "col", split_axis=3, concat_axis=4, tiled=True)
    full_spec = jnp.einsum("fpdxz,dzck->fpxck", returned, span_out, precision=PRECISE)
    home = lax.all_to_all(full_spec, "row", split_axis=4, concat_axis=1, tiled=True)
    h_x = split_pair(home[0])
    h_y = split_pair(home[1])
    h_z = split_pair(home[2])
    square = stream_here * stream_here + span_here * span_here
    g_term = combine(rotate(h_x, span_here), rotate(h_z, stream_here), -1.0)
    s_term = scaled(combine(rotate(h_x, stream_here), rotate(h_z, span_here), 1.0), -1.0)
    y_term = scaled(h_y, -square)
    damp_g = 1.0 / jnp.sqrt(1.0 + square)
    damp_v = 1.0 / (1.0 + square)

    def contract(matrix, term):
        return jnp.einsum("jp,pxck->cxkj", matrix, join_pair(term), precision=PRECISE)

    vort_rhs = contract(inverse_ops[0], g_term) * damp_g[None, :, :, None]
    lapv_sum = contract(inverse_ops[1], s_term) + contract(inverse_ops[0], y_term)
    lapv_rhs = lapv_sum * damp_v[None, :, :, None]
    return (vort_rhs, lapv_rhs)


def solution(mesh):
    in_specs = (P(None, "col", "row", None), P(None, "col", "row", None), P(), P())
    out_specs = (P(None, "col", "row", None), P(None, "col", "row", None))
    sizes = {"row": mesh.shape["row"], "col": mesh.shape["col"]}

    def choose(v_coef, vort_coef, plane_ops, inverse_ops):
        args = (v_coef, vort_coef, plane_ops, inverse_ops)
        fits = (
            2 * v_coef.shape[1] == LANES
            and v_coef.shape[2] % 32 == 0
            and v_coef.shape[3] == 2 * LANES
            and plane_ops.shape[1] % sizes["row"] == 0
            and plane_ops.shape[1] <= 12
            and sizes["col"] == 8
        )
        return per_device_fast(*args, sizes) if fits else per_device(*args)

    return jax.shard_map(choose, mesh=mesh, in_specs=in_specs, out_specs=out_specs, check_vma=False)
```

```python
import functools
import math

import jax
import jax.numpy as jnp
import ml_dtypes
import numpy as np
from jax import lax
from jax.experimental import pallas as pl
from jax.experimental.pallas import tpu as pltpu
from jax.sharding import PartitionSpec as P

PRECISE = lax.Precision.HIGHEST
STREAM_STEP = 0.25
SPAN_STEP = 2.0 / 3.0
INVERSE_SCALE = 1.0 / 32.0
FORWARD_SCALE = 32.0
LANES = 128
VMEM_LIMIT = 26 * 1024 * 1024
MESH = pl.DeviceIdType.MESH
F32 = jnp.float32
BF16 = jnp.bfloat16


def halves(table):
    table = np.asarray(table, np.float32)
    high = table.astype(ml_dtypes.bfloat16)
    low = (table - high.astype(np.float32)).astype(ml_dtypes.bfloat16)
    return np.stack([high, low], axis=0)


def signed_order(rows, span_local, span_total):
    n = (
        span_local * np.arange(rows)[:, None, None]
        + np.arange(2)[None, :, None]
        + 2 * np.arange(span_local // 2)[None, None, :]
    )
    return np.where(n < span_total // 2, n, n - span_total)


def span_fast_tables(rows, span_local, span_total):
    points = 3 * span_total // 2
    signed = signed_order(rows, span_local, span_total)
    grid = np.arange(points // 2)
    inverse, forward = [], []
    for parity in range(2):
        s = signed[:, parity, :].reshape(-1)
        angle = np.mod(s[None, :] * grid[:, None], points) * (2.0 * math.pi / points)
        inverse.append(np.concatenate([np.cos(angle), np.sin(angle)], axis=1))
        factor = FORWARD_SCALE / points
        forward.append(np.concatenate([np.cos(angle).T, np.sin(angle).T], axis=1) * factor)
    return halves(np.stack(inverse)), halves(np.stack(forward))


def stream_fast_tables(total):
    points = 3 * total
    grid = np.arange(points // 4) + 0.5
    inverse, forward = [], []
    for part in range(2):
        for parity in range(2):
            m = 2 * np.arange(total // 2) + parity
            angle = np.mod(m[:, None] * grid[None, :], points) * (2.0 * math.pi / points)
            wave = np.cos(angle) if part == 0 else -np.sin(angle)
            weight = np.where(m == 0, 1.0, 2.0)[:, None]
            inverse.append(weight * wave * INVERSE_SCALE)
            forward.append(wave.T / points)
    return halves(np.stack(inverse)), halves(np.stack(forward))


def split(values):
    high = values.astype(BF16)
    return high, (values - high.astype(F32)).astype(BF16)


def dot(a, b):
    return jnp.dot(a, b, preferred_element_type=F32)


def dot3(a_high, a_low, b_high, b_low):
    return dot(a_high, b_high) + (dot(a_high, b_low) + dot(a_low, b_high))


def times_i(values):
    axis = values.ndim - 1
    lane = lax.broadcasted_iota(jnp.int32, values.shape, axis)
    turned = pltpu.roll(values, LANES // 2, axis)
    return jnp.where(lane < LANES // 2, -turned, turned)


def block_transpose(a):
    lane = lax.broadcasted_iota(jnp.int32, a[0].shape, 1)
    left = lane < 64
    odd = (lane // 32) % 2 == 1
    t = [None] * 4
    for s in range(2):
        t[s] = jnp.where(left, a[s], pltpu.roll(a[s + 2], 64, 1))
        t[s + 2] = jnp.where(left, pltpu.roll(a[s], 64, 1), a[s + 2])
    out = [None] * 4
    for s in (0, 2):
        out[s] = jnp.where(odd, pltpu.roll(t[s + 1], 32, 1), t[s])
        out[s + 1] = jnp.where(odd, t[s + 1], pltpu.roll(t[s], 96, 1))
    return out


def contract_last(a, b):
    return lax.dot_general(a, b, (((1,), (1,)), ((), ())), preferred_element_type=F32)


def plane_kernel(
    v_ref, g_ref, first_ref, second_ref, out_ref, held_ref,
    y_ref, staged, send_sem, recv_sem, local_sem, *, rows_count, steps
):
    used = out_ref.shape[0]
    count = used // 5
    step = pl.program_id(0)
    me, col = lax.axis_index("row"), lax.axis_index("col")
    peers = [lax.rem(me + offset, rows_count) for offset in range(1, rows_count)]

    @pl.when(step == 0)
    def _():
        barrier = pltpu.get_barrier_semaphore()
        for peer in peers:
            pl.semaphore_signal(barrier, inc=1, device_id=(peer, col), device_id_type=MESH)
        pl.semaphore_wait(barrier, rows_count - 1)

    def sent(index, slot):
        at = pl.ds(pl.multiple_of(index * 8, 8), 8)
        return pltpu.make_async_remote_copy(
            src_ref=staged.at[peers[slot], :, :, at],
            dst_ref=held_ref.at[me, :, :, at],
            send_sem=send_sem.at[index, slot],
            recv_sem=recv_sem.at[index, slot],
            device_id=(peers[slot], col),
            device_id_type=MESH,
        )

    flat = out_ref.reshape(used * 16, LANES)
    for part in range(2):
        for side in range(2):
            at = pl.ds(side * 32, 32)
            rows = [ref[part, at].reshape(512, 2 * LANES) for ref in (v_ref, g_ref)]
            high, low = split(jnp.concatenate(rows, axis=1))
            y = dot(high, first_ref[...])
            y = y + pltpu.roll(y, LANES // 2, 1) + dot(low, second_ref[...])
            y_ref[pl.ds((2 * part + side) * 512, 512), :] = y
    for parity in range(2):
        for half in range(8):
            rows = []
            for part in range(2):
                for odd in range(2):
                    start = part * 1024 + odd * 16 + 2 * half + parity
                    rows.append(y_ref[pl.ds(start, 32, stride=32), :])
            turned = jnp.concatenate(rows, axis=0).T
            flat[pl.ds(parity * 8 + half, used, stride=16), :] = turned[:used]
    here = pl.ds(pl.multiple_of(step * 8, 8), 8)
    for row in range(rows_count):
        for r in range(5):
            staged[row, r, :, here] = out_ref[r * count + row]
    for slot in range(rows_count - 1):
        sent(step, slot).start()

    @pl.when(step == steps - 1)
    def _():
        own = pltpu.make_async_copy(staged.at[me], held_ref.at[me], local_sem)
        own.start()

        @pl.loop(0, steps)
        def _(index):
            for slot in range(rows_count - 1):
                sent(index, slot).wait()

        own.wait()


def span_inverse_kernel(r_ref, kx_ref, kz_ref, t_ref, out_ref, high_ref, low_ref, *, rows, half):
    modes = rows * half

    @pl.when(pl.program_id(0) == 0)
    def _():
        kx = kx_ref[...]
        for row in range(rows):
            for parity in range(2):
                kz = kz_ref[row, parity]
                square = kx * kx + kz * kz
                recip = 1.0 / jnp.where(square > 0, square, 1.0)
                vb, vd, vdd, gb, gd = [r_ref[row, f, parity] for f in range(5)]
                members = [
                    times_i((kx * vd - kz * gb) * recip),
                    vb,
                    times_i((kz * vd + kx * gb) * recip),
                    times_i((kz * vdd + kx * gd) * recip - kz * vb),
                    gb,
                    times_i(kx * vb - (kx * vdd - kz * gd) * recip),
                ]
                for f, member in enumerate(members):
                    for place, values in ((0, member), (modes, times_i(member))):
                        high, low = split(values)
                        at = pl.ds(place + row * half, half)
                        high_ref[f // 2, parity, at, pl.ds((f % 2) * LANES, LANES)] = high
                        low_ref[f // 2, parity, at, pl.ds((f % 2) * LANES, LANES)] = low

    pair = pl.program_id(0)
    even, odd = [
        dot3(t_ref[0, q], t_ref[1, q], high_ref[pair, q], low_ref[pair, q]) for q in range(2)
    ]
    plus, minus = even + odd, even - odd
    dests = out_ref.shape[0]
    step = out_ref.shape[2] // 2
    for d in range(dests):
        for f in range(2):
            lanes = slice(f * LANES, (f + 1) * LANES)
            out_ref[d, f, :step] = plus[d * step : (d + 1) * step, lanes]
            out_ref[d, f, step:] = minus[d * step : (d + 1) * step, lanes]


def stream_kernel(x_ref, ti_ref, tf_ref, out_ref):
    sources, fields, block, _ = x_ref.shape
    width = ti_ref.shape[3]
    parts = [x_ref[s].reshape(fields * block, LANES) for s in range(sources)]
    groups = [[] for _ in range(4)]
    for s in range(0, sources, 4):
        for g, piece in enumerate(block_transpose(parts[s : s + 4])):
            groups[g].append(piece)
    spectral = []
    for g in range(4):
        high, low = split(jnp.concatenate(groups[g], axis=1))
        spectral.append(dot3(high, low, ti_ref[0, g], ti_ref[1, g]))
    ce, co, se, so = [s.reshape(fields, block, width) for s in spectral]
    a, b, c, d = ce + co, se + so, ce - co, se - so
    products = []
    for image in (a + b, a - b, c + d, c - d):
        u, v, w, ox, oy, oz = [image[f] for f in range(6)]
        products.append(jnp.stack([v * oz - w * oy, w * ox - u * oz, u * oy - v * ox], axis=0))
    h1, h2, h3, h4 = [h.reshape(3 * block, width) for h in products]
    sum1, sum2, dif1, dif2 = h1 + h2, h3 + h4, h1 - h2, h3 - h4
    results = []
    for g, h in enumerate((sum1 + sum2, sum1 - sum2, dif1 + dif2, dif1 - dif2)):
        high, low = split(h)
        results.append(dot3(high, low, tf_ref[0, g], tf_ref[1, g]))
    for s in range(0, sources, 4):
        at = (s // 4) * LANES
        pieces = block_transpose([r[:, at : at + LANES] for r in results])
        for k in range(4):
            out_ref[s + k] = pieces[k].reshape(3, block, LANES)


def span_forward_kernel(x_ref, t_ref, out_ref):
    sources, fields, both, _ = x_ref.shape
    step = both // 2
    rows, half = out_ref.shape[0], out_ref.shape[3]
    for parity in range(2):
        columns = []
        for f in range(fields):
            first, second = x_ref[:, f, :step], x_ref[:, f, step:]
            h = first + second if parity == 0 else first - second
            h = h.reshape(sources * step, LANES)
            columns.append(jnp.concatenate([h, -times_i(h)], axis=0))
        high, low = split(jnp.concatenate(columns, axis=1))
        result = dot3(t_ref[0, parity], t_ref[1, parity], high, low)
        for row in range(rows):
            for f in range(fields):
                out_ref[row, f, parity] = result[
                    row * half : (row + 1) * half, f * LANES : (f + 1) * LANES
                ]


def combine_kernel(*refs, chunks, rows, count):
    h_refs = refs[:chunks]
    kx_ref, kz_ref, w_ref, vort_ref, lapv_ref, terms, left = refs[chunks:]
    kx = kx_ref[...]
    padded = terms.shape[0] // 16
    if padded > 3 * count:
        terms[3 * count * 16 :, :] = jnp.zeros(((padded - 3 * count) * 16, LANES), F32)
    for parity in range(2):
        kz = kz_ref[parity]
        square = kx * kx + kz * kz
        damp_g = 1.0 / jnp.sqrt(1.0 + square)
        damp_v = 1.0 / (1.0 + square)
        for chunk in range(chunks):
            for row in range(rows):
                p = chunk * rows + row
                hx, hy, hz = [h_refs[chunk][row, f, parity] for f in range(3)]
                members = (
                    times_i(kz * hx - kx * hz) * damp_g,
                    -times_i(kx * hx + kz * hz) * damp_v,
                    -square * hy * damp_v,
                )
                for t, member in enumerate(members):
                    at = (t * count + p) * 16 + parity * 8
                    terms[at : at + 8, :] = member
    for parity in range(2):
        for half in range(8):
            values = terms[pl.ds(parity * 8 + half, padded, stride=16), :]
            high = values.astype(BF16).astype(F32)
            rest = jnp.zeros((LANES - 3 * padded, LANES), F32)
            turned = jnp.concatenate([high, values - high, high, rest], axis=0).T
            for part in range(2):
                for odd in range(2):
                    start = part * 1024 + odd * 16 + 2 * half + parity
                    at = part * 64 + odd * 32
                    left[pl.ds(start, 32, stride=32), :] = turned[at : at + 32]
    for part in range(2):
        for side in range(2):
            rows = left[pl.ds((2 * part + side) * 512, 512), :].astype(BF16)
            result = dot(rows, w_ref[...]).reshape(32, 16, 4 * LANES)
            vort_ref[part, pl.ds(side * 32, 32)] = result[:, :, : 2 * LANES]
            lapv_ref[part, pl.ds(side * 32, 32)] = result[:, :, 2 * LANES :]


def exchange_kernel(*refs, jobs, sizes):
    count = len(jobs)
    sources, dests = refs[:count], refs[count : 2 * count]
    send_sem, recv_sem, local_sem = refs[2 * count :]
    position = {axis: lax.axis_index(axis) for axis in ("row", "col")}
    axes = sorted({axis for axis, _ in jobs})
    barrier = pltpu.get_barrier_semaphore()

    def target(axis, offset):
        return lax.rem(position[axis] + offset, sizes[axis])

    def device(axis, index):
        return (index, position["col"]) if axis == "row" else (position["row"], index)

    total = 0
    for axis in axes:
        for offset in range(1, sizes[axis]):
            total += 1
            pl.semaphore_signal(
                barrier,
                inc=1,
                device_id=device(axis, target(axis, offset)),
                device_id_type=MESH,
            )
    pl.semaphore_wait(barrier, total)

    def block(ref, axis, chunk, index):
        return ref.at[index] if chunk is None else ref.at[:, chunk * sizes[axis] + index]

    copies = []
    slot = 0
    for job, (axis, chunk) in enumerate(jobs):
        me = position[axis]
        for offset in range(1, sizes[axis]):
            peer = target(axis, offset)
            copy = pltpu.make_async_remote_copy(
                src_ref=block(sources[job], axis, chunk, peer),
                dst_ref=dests[job].at[me],
                send_sem=send_sem.at[slot],
                recv_sem=recv_sem.at[slot],
                device_id=device(axis, peer),
                device_id_type=MESH,
            )
            copy.start()
            copies.append(copy)
            slot += 1
    for job, (axis, chunk) in enumerate(jobs):
        me = position[axis]
        own = pltpu.make_async_copy(
            block(sources[job], axis, chunk, me), dests[job].at[me], local_sem.at[job]
        )
        own.start()
        copies.append(own)
    for copy in copies:
        copy.wait()


def exchange(jobs, arrays, sizes, collective_id):
    shapes = []
    for (axis, chunk), array in zip(jobs, arrays):
        shape = array.shape
        if chunk is not None:
            shape = (sizes[axis], shape[0]) + shape[2:]
        shapes.append(jax.ShapeDtypeStruct(shape, array.dtype))
    slots = sum(sizes[axis] - 1 for axis, _ in jobs)
    anywhere = pl.BlockSpec(memory_space=pl.ANY)
    return pl.pallas_call(
        functools.partial(exchange_kernel, jobs=tuple(jobs), sizes=sizes),
        out_shape=shapes,
        in_specs=[anywhere] * len(jobs),
        out_specs=[anywhere] * len(jobs),
        scratch_shapes=[
            pltpu.SemaphoreType.DMA((slots,)),
            pltpu.SemaphoreType.DMA((slots,)),
            pltpu.SemaphoreType.DMA((len(jobs),)),
        ],
        compiler_params=pltpu.CompilerParams(collective_id=collective_id, has_side_effects=True),
        name="exchange_%d" % collective_id,
    )(*arrays)


def rounded_halves(w):
    high = lax.reduce_precision(w, 8, 7)
    return high.astype(BF16), (w - high).astype(BF16)


def pad_rows(w, rows):
    return jnp.pad(w, ((0, rows - w.shape[0]), (0, 0)))


def params(**extra):
    return pltpu.CompilerParams(vmem_limit_bytes=VMEM_LIMIT, **extra)


def whole(shape):
    return pl.BlockSpec(shape, lambda *_: (0,) * len(shape))


def per_device_fast(v_coef, vort_coef, plane_ops, inverse_ops, sizes):
    rows, cols = sizes["row"], sizes["col"]
    _, stream_local, span_local, coefs = v_coef.shape
    count = plane_ops.shape[1]
    chunks = count // rows
    half = span_local // 2
    modes = rows * half
    stream_total, span_total = stream_local * cols, span_local * rows
    points = 3 * span_total // 2
    step = points // (2 * cols)
    stream_points = 3 * stream_total

    lane = jnp.arange(LANES, dtype=jnp.int32)
    mode = 2 * (lane % 32) + (lane // 32) % 2 + stream_local * lax.axis_index("col")
    kx = (STREAM_STEP * mode.astype(F32))[None, :]
    signed = signed_order(rows, span_local, span_total)
    kz_all = np.broadcast_to(
        (np.float32(SPAN_STEP) * signed.astype(np.float32))[..., None], signed.shape + (LANES,)
    )
    n_here = (
        span_local * lax.axis_index("row")
        + jnp.arange(2, dtype=jnp.int32)[:, None]
        + 2 * jnp.arange(half, dtype=jnp.int32)[None, :]
    )
    signed_here = jnp.where(n_here < span_total // 2, n_here, n_here - span_total)
    kz_here = jnp.broadcast_to(
        (SPAN_STEP * signed_here.astype(F32))[..., None], (2, half, LANES)
    )
    span_in, span_out = span_fast_tables(rows, span_local, span_total)
    stream_in, stream_out = stream_fast_tables(stream_total)

    used = 5 * count
    highs, lows = [], []
    for ops, before, after in ((plane_ops, 0, 2), (plane_ops[:2], 3, 0)):
        flat = ops.reshape(-1, coefs).T
        for kept, w in zip((highs, lows), rounded_halves(flat)):
            kept.append(jnp.pad(w, ((0, 0), (before * count, after * count + 64 - used))))
    high, low = [jnp.concatenate(kept, axis=0) for kept in (highs, lows)]
    weights = [
        jnp.concatenate([high, low], axis=1),
        jnp.concatenate([high, jnp.zeros_like(high)], axis=1),
    ]

    coef_spec = pl.BlockSpec((2, stream_local, 16, coefs), lambda i: (0, 0, i, 0))
    steps = span_local // 16
    values, held = pl.pallas_call(
        functools.partial(plane_kernel, rows_count=rows, steps=steps),
        grid=(steps,),
        out_shape=[
            jax.ShapeDtypeStruct((used, 2, half, LANES), F32),
            jax.ShapeDtypeStruct((rows, 5, 2, half, LANES), F32),
        ],
        in_specs=[coef_spec] * 2 + [whole(w.shape) for w in weights],
        out_specs=[
            pl.BlockSpec((used, 2, 8, LANES), lambda i: (0, 0, i, 0)),
            pl.BlockSpec(memory_space=pl.ANY),
        ],
        scratch_shapes=[
            pltpu.VMEM((2 * stream_local * 16, LANES), F32),
            pltpu.VMEM((rows, 5, 2, half, LANES), F32),
            pltpu.SemaphoreType.DMA((steps, rows - 1)),
            pltpu.SemaphoreType.DMA((steps, rows - 1)),
            pltpu.SemaphoreType.DMA,
        ],
        compiler_params=params(collective_id=0, has_side_effects=True),
        name="plane_values",
    )(v_coef, vort_coef, *weights)
    values = values.reshape(5, count, 2, half, LANES)

    def span_inverse(received):
        return pl.pallas_call(
            functools.partial(span_inverse_kernel, rows=rows, half=half),
            grid=(3,),
            out_shape=jax.ShapeDtypeStruct((cols, 6, 2 * step, LANES), F32),
            in_specs=[
                whole((rows, 5, 2, half, LANES)),
                whole((1, LANES)),
                whole(kz_all.shape),
                whole(span_in.shape),
            ],
            out_specs=pl.BlockSpec((cols, 2, 2 * step, LANES), lambda i: (0, i, 0, 0)),
            scratch_shapes=[pltpu.VMEM((3, 2, 2 * modes, 2 * LANES), BF16)] * 2,
            compiler_params=params(),
            name="span_inverse",
        )(received, kx, jnp.asarray(kz_all), jnp.asarray(span_in))

    def stream_products(arrived):
        block = 48
        return pl.pallas_call(
            stream_kernel,
            grid=(2 * step // block,),
            out_shape=jax.ShapeDtypeStruct((cols, 3, 2 * step, LANES), F32),
            in_specs=[
                pl.BlockSpec((cols, 6, block, LANES), lambda i: (0, 0, i, 0)),
                whole(stream_in.shape),
                whole(stream_out.shape),
            ],
            out_specs=pl.BlockSpec((cols, 3, block, LANES), lambda i: (0, 0, i, 0)),
            compiler_params=params(),
            name="stream_products",
        )(arrived, jnp.asarray(stream_in), jnp.asarray(stream_out))

    def span_forward(returned):
        return pl.pallas_call(
            span_forward_kernel,
            out_shape=jax.ShapeDtypeStruct((rows, 3, 2, half, LANES), F32),
            compiler_params=params(),
            name="span_forward",
        )(returned, jnp.asarray(span_out))

    state = [values] * chunks
    after = [span_inverse, stream_products, span_forward, lambda home: home]
    axes = ["row", "col", "col", "row"]
    state[0] = span_inverse(held)
    for turn in range(1, chunks + 3):
        active = [c for c in range(chunks) if 0 <= turn - c < 4]
        jobs = [(axes[turn - c], c if turn == c else None) for c in active]
        results = exchange(jobs, [state[c] for c in active], sizes, turn)
        for c, result in zip(active, results):
            state[c] = after[turn - c](result)

    inv0, inv1 = inverse_ops[0].T, inverse_ops[1].T
    none = jnp.zeros_like(inv0)
    table = jnp.concatenate(
        [
            jnp.concatenate([inv0, none], axis=1),
            jnp.concatenate([none, inv1], axis=1),
            jnp.concatenate([none, inv0], axis=1),
        ],
        axis=0,
    )
    padded = -(-3 * count // 8) * 8
    high, low = [pad_rows(w, padded) for w in rounded_halves(table)]
    table = pad_rows(jnp.concatenate([high, high, low], axis=0), LANES)
    out_block = pl.BlockSpec((2, stream_local, 16, coefs), lambda i: (0, 0, i, 0))
    return pl.pallas_call(
        functools.partial(combine_kernel, chunks=chunks, rows=rows, count=count),
        grid=(span_local // 16,),
        out_shape=[jax.ShapeDtypeStruct(v_coef.shape, F32)] * 2,
        in_specs=[pl.BlockSpec((rows, 3, 2, 8, LANES), lambda i: (0, 0, 0, i, 0))] * chunks
        + [
            whole((1, LANES)),
            pl.BlockSpec((2, 8, LANES), lambda i: (0, i, 0)),
            whole(table.shape),
        ],
        out_specs=[out_block] * 2,
        scratch_shapes=[pltpu.VMEM((padded * 16, LANES), F32)]
        + [pltpu.VMEM((2 * stream_local * 16, LANES), F32)],
        compiler_params=params(),
        name="combinations",
    )(*state, kx, kz_here, table)


def signed_modes(first, count, total):
    modes = first + jnp.arange(count, dtype=jnp.int32)
    return jnp.where(modes < total // 2, modes, modes - total)


def span_tables(total):
    points = 3 * total // 2
    n = np.arange(total)
    signed = np.where(n < total // 2, n, n - total)
    angle = np.mod(signed[:, None] * np.arange(points)[None, :], points) * (2.0 * math.pi / points)
    cosine, sine = np.cos(angle), np.sin(angle)
    inverse = np.stack(
        [np.stack([cosine, sine], axis=1), np.stack([-sine, cosine], axis=1)], axis=0
    )
    forward = np.stack(
        [np.stack([cosine.T, -sine.T], axis=1), np.stack([sine.T, cosine.T], axis=1)], axis=0
    ) * (FORWARD_SCALE / points)
    return jnp.asarray(inverse, F32), jnp.asarray(forward, F32)


def stream_tables(total):
    points = 3 * total
    modes = np.arange(total)
    angle = np.mod(modes[:, None] * np.arange(points)[None, :], points) * (2.0 * math.pi / points)
    cosine, sine = np.cos(angle), np.sin(angle)
    weights = np.where(modes == 0, 1.0, 2.0)[:, None]
    inverse = np.stack([weights * cosine, -weights * sine], axis=0) * INVERSE_SCALE
    forward = np.stack([cosine.T, -sine.T], axis=1) / points
    return jnp.asarray(inverse, F32), jnp.asarray(forward, F32)


def rotate(pair, factor):
    return (-factor * pair[1], factor * pair[0])


def combine(first, second, sign):
    return (first[0] + sign * second[0], first[1] + sign * second[1])


def scaled(pair, factor):
    return (pair[0] * factor, pair[1] * factor)


def split_pair(values):
    return (values[..., 0, :], values[..., 1, :])


def join_pair(pair):
    return jnp.stack(pair, axis=-2)


def build_fields(values, stream, span):
    v_base = split_pair(values[0])
    v_slope = split_pair(values[1])
    v_curve = split_pair(values[2])
    g_base = split_pair(values[3])
    g_slope = split_pair(values[4])
    square = stream * stream + span * span
    recip = 1.0 / jnp.where(square > 0, square, 1.0)
    along = scaled(combine(rotate(v_slope, stream), rotate(g_base, span), -1.0), recip)
    across = scaled(combine(rotate(v_slope, span), rotate(g_base, stream), 1.0), recip)
    omega_x = combine(
        scaled(combine(rotate(v_curve, span), rotate(g_slope, stream), 1.0), recip),
        rotate(v_base, span),
        -1.0,
    )
    omega_z = combine(
        rotate(v_base, stream),
        scaled(combine(rotate(v_curve, stream), rotate(g_slope, span), -1.0), recip),
        -1.0,
    )
    group_members = [along, v_base, across, omega_x, g_base, omega_z]
    return jnp.stack([join_pair(member) for member in group_members], axis=0)


def per_device(v_coef, vort_coef, plane_ops, inverse_ops):
    row_count = lax.axis_size("row")
    column_total_count = lax.axis_size("col")
    stream_local = v_coef.shape[1]
    span_local = v_coef.shape[2]
    stream_total = stream_local * column_total_count
    span_total = span_local * row_count
    stream_first = lax.axis_index("col") * stream_local
    span_first = lax.axis_index("row") * span_local
    stream_here = (
        STREAM_STEP * (stream_first + jnp.arange(stream_local, dtype=jnp.int32)).astype(jnp.float32)
    )[:, None]
    span_here = (SPAN_STEP * signed_modes(span_first, span_local, span_total).astype(jnp.float32))[
        None, :
    ]
    span_in, span_out = span_tables(span_total)
    stream_in, stream_out = stream_tables(stream_total)
    v_values = jnp.einsum("rpj,cxkj->rpxck", plane_ops, v_coef, precision=PRECISE)
    g_values = jnp.einsum("rpj,cxkj->rpxck", plane_ops[:2], vort_coef, precision=PRECISE)
    values = jnp.concatenate([v_values, g_values], axis=0)
    fields = build_fields(values, stream_here, span_here)
    pencils = lax.all_to_all(fields, "row", split_axis=1, concat_axis=4, tiled=True)
    span_phys = jnp.einsum("fpxck,ckdz->fpdxz", pencils, span_in, precision=PRECISE)
    arrived = lax.all_to_all(span_phys, "col", split_axis=4, concat_axis=3, tiled=True)
    physical = jnp.einsum("fpcmz,cmx->fpzx", arrived, stream_in, precision=PRECISE)
    velocity = physical[0:3]
    vorticity = physical[3:6]
    product_streamwise = velocity[1] * vorticity[2] - velocity[2] * vorticity[1]
    product_normal = velocity[2] * vorticity[0] - velocity[0] * vorticity[2]
    product_spanwise = velocity[0] * vorticity[1] - velocity[1] * vorticity[0]
    products = jnp.stack([product_streamwise, product_normal, product_spanwise], axis=0)
    stream_spec = jnp.einsum("fpzx,xcm->fpcmz", products, stream_out, precision=PRECISE)
    returned = lax.all_to_all(stream_spec, "col", split_axis=3, concat_axis=4, tiled=True)
    full_spec = jnp.einsum("fpdxz,dzck->fpxck", returned, span_out, precision=PRECISE)
    home = lax.all_to_all(full_spec, "row", split_axis=4, concat_axis=1, tiled=True)
    h_x = split_pair(home[0])
    h_y = split_pair(home[1])
    h_z = split_pair(home[2])
    square = stream_here * stream_here + span_here * span_here
    g_term = combine(rotate(h_x, span_here), rotate(h_z, stream_here), -1.0)
    s_term = scaled(combine(rotate(h_x, stream_here), rotate(h_z, span_here), 1.0), -1.0)
    y_term = scaled(h_y, -square)
    damp_g = 1.0 / jnp.sqrt(1.0 + square)
    damp_v = 1.0 / (1.0 + square)

    def contract(matrix, term):
        return jnp.einsum("jp,pxck->cxkj", matrix, join_pair(term), precision=PRECISE)

    vort_rhs = contract(inverse_ops[0], g_term) * damp_g[None, :, :, None]
    lapv_sum = contract(inverse_ops[1], s_term) + contract(inverse_ops[0], y_term)
    lapv_rhs = lapv_sum * damp_v[None, :, :, None]
    return (vort_rhs, lapv_rhs)


def solution(mesh):
    in_specs = (P(None, "col", "row", None), P(None, "col", "row", None), P(), P())
    out_specs = (P(None, "col", "row", None), P(None, "col", "row", None))
    sizes = {"row": mesh.shape["row"], "col": mesh.shape["col"]}

    def choose(v_coef, vort_coef, plane_ops, inverse_ops):
        args = (v_coef, vort_coef, plane_ops, inverse_ops)
        fits = (
            2 * v_coef.shape[1] == LANES
            and v_coef.shape[2] % 32 == 0
            and v_coef.shape[3] == 2 * LANES
            and plane_ops.shape[1] % sizes["row"] == 0
            and plane_ops.shape[1] <= 12
            and sizes["col"] == 8
        )
        return per_device_fast(*args, sizes) if fits else per_device(*args)

    return jax.shard_map(choose, mesh=mesh, in_specs=in_specs, out_specs=out_specs, check_vma=False)
```
